32 devices in a mesh: runs: 2 (over y), tensor: 16 (over z, x, core).
Axes of the slice: x: 2, y: 2, z: 4, core: 2. Of those that a mesh axis runs over, the one named last changes fastest.
Arguments:
- activations: bfloat16 [64, 512, 28672], P('runs', None, 'tensor'), parts along dimension 0, may hold values from -6 to 6
- output_gradient_rows: bfloat16 [64, 512, 8192], P('runs', None, 'tensor'), parts along dimension 0, may hold values from -6 to 6
- factor_in: bfloat16 [32, 32, 28672], P('runs', None, 'tensor'), parts along dimension 0, may hold values from -0.015625 to 0.015625
- factor_out: bfloat16 [32, 32, 8192], P('runs', None, 'tensor'), parts along dimension 0, may hold values from -0.02734375 to 0.02734375
- list_counts: int32 [32], P('runs'), parts along dimension 0, may hold values from 1 to 4, 40 in all
- list_seqs: int32 [32, 4], P('runs'), parts along dimension 0, may hold values from 0 to 31
Outputs:
- scores: float32 [512, 128], P('tensor', 'runs'), parts along dimension 1
- totals: float32 [32], P('runs'), parts along dimension 0
The draws below stay inside these ranges and needn't reach their ends.
There are 2 independent parts, one for each index of `runs`. The reference program is written for one: setup_inputs(seed, part) draws one part's arguments, and reference() takes and returns one part's arrays. A program takes and returns all parts, laid end to end along the dimension named above; each array names one. Nothing has to cross between parts.
Inputs may be any that keep to these rules, and one draw needn't show every extreme that they name: `list_counts`: each query lists 1 to 4 sequences, 40 in all; some query lists exactly 4. `list_seqs`: sequence ids; only the first list_counts[q] slots of query q are read.
All inputs are finite; a program needn't handle non-finite values.
Results may differ from the reference program's by a relative error of at most 0.0003.
Values sent between devices are 32-bit elements; how exact they have to be, the bound alone decides.
No kernel may reach another device: no remote copies, remote signals or barrier semaphores. Data moves between devices by JAX's collectives and lax.ppermute only.
A program may use at most 256 MiB of HBM per device.

```python
import math
import jax
import jax.numpy as jnp
import numpy as np
from jax import lax

D = 8192
FF = 28672
RANK = 32
SEQ_LEN = 512
QW = 16
NSEQ = 32
KMAX = 4
PAIRS = 40


def set_ends(drawn, key, smallest, high):
    extent = drawn.shape
    index_at = [jax.random.randint(jax.random.fold_in(key, axis), (), 0, extent[axis]) for axis in range(len(extent))]
    drawn = drawn.at[tuple(index_at)].set(smallest)
    longest = extent.index(max(extent))
    index_at[longest] = (index_at[longest] + 1) % extent[longest]
    return drawn.at[tuple(index_at)].set(high)


def raised(entries, rng, source, target, shards_of, factor):
    def block_of(position):
        return (jnp.arange(entries.shape[position]) // (entries.shape[position] // shards_of)).reshape((-1,) + (1,) * (entries.ndim - 1 - position))

    near = jax.random.permutation(rng, shards_of)[block_of(target)]
    far = (block_of(target) + shards_of // 2) % shards_of
    return jnp.where((block_of(source) == near) | (block_of(source) == far), factor * entries, entries)


def shard_levels(key, extent, shards, least, top_value):
    level = 1.0
    for dim, parts in shards:
        draws = jax.random.uniform(jax.random.fold_in(jax.random.fold_in(key, 6), dim), (parts,), jnp.float32, least / len(shards), top_value / len(shards))
        level = level * jnp.repeat(jnp.exp(draws), extent[dim] // parts).reshape((-1,) + (1,) * (len(extent) - 1 - dim))
    return level


def profile(amount, total, limit, lean):
    portions = [(1 << 20) // math.isqrt(rank ** lean) + 1 for rank in range(2, amount + 1)]
    rest, holding = total - limit - (amount - 1), [1] * (amount - 1)
    while rest > 0:
        movable = [i for i in range(amount - 1) if holding[i] < limit]
        pool, budget = sum([portions[i] for i in movable]), rest
        for i in movable:
            more = min(limit - holding[i], max(1, budget * portions[i] // pool), rest)
            holding[i] = holding[i] + more
            rest = rest - more
    return np.array([limit] + holding)


def uneven(own_key, count, total, bound, skew):
    if count == 2:
        one = jax.random.randint(own_key, (), max(1, total - bound), min(bound, total - 1) + 1)
        return jnp.stack([one, total - one])
    sizes = jnp.asarray(profile(count, total, bound, skew), jnp.int32)
    twos = (count - 1) // 2
    giver, sink = sizes[1:1 + 2 * twos:2], sizes[2:2 + 2 * twos:2]
    room = jnp.minimum(giver - 1, bound - sink)
    shifted = jax.random.randint(jax.random.fold_in(own_key, 1), (twos,), 0, 1 << 20) % (room + 1)
    sizes = sizes.at[1:1 + 2 * twos:2].set(giver - shifted).at[2:2 + 2 * twos:2].set(sink + shifted)
    return sizes[jax.random.permutation(jax.random.fold_in(own_key, 2), count)]


def centred(own_key, extent, width, limit, split=(), held_as=jnp.bfloat16):
    drawn = width * jax.random.normal(own_key, extent, jnp.float32)
    if split:
        drawn = drawn * shard_levels(own_key, extent, split, -0.22, 0.18)
    return jnp.clip(drawn, -limit, limit).astype(held_as)


def bell_draw_with(stream_key, shape, scale, limit, shards, heavy, held_as=jnp.bfloat16):
    result = scale * jax.random.normal(stream_key, shape, jnp.float32)
    if shards:
        result = result * shard_levels(stream_key, shape, shards, -0.22, 0.18)
    return jnp.clip(raised(result, jax.random.fold_in(stream_key, 3), *heavy), -limit, limit).astype(held_as)


def setup_inputs(seed: int = 0, part: int = 0) -> dict:
    key_list = jax.random.split(jax.random.key(seed), 7)
    own_keys = jax.random.split(jax.random.fold_in(key_list[6], part), 7)
    activations = bell_draw_with(own_keys[0], (NSEQ, SEQ_LEN, FF), 1.0, 6.0, ((2, 16),), (2, 1, 16, 2.0))
    output_gradient_rows = bell_draw_with(own_keys[1], (NSEQ, SEQ_LEN, D), 1.0, 6.0, ((2, 16),), (2, 1, 16, 2.0))
    factor_in = centred(own_keys[2], (QW, RANK, FF), (6 * FF) ** -0.5, 0.015625, ((2, 16),))
    factor_out = centred(own_keys[3], (QW, RANK, D), (6 * D) ** -0.5, 0.02734375, ((2, 16),))
    list_counts = uneven(own_keys[4], QW, PAIRS, KMAX, 2).astype(jnp.int32)
    list_seqs = set_ends(jax.random.randint(own_keys[5], (QW, KMAX), 0, NSEQ), jax.random.fold_in(own_keys[5], 1), 0, NSEQ - 1).astype(jnp.int32)
    return dict(activations=activations, output_gradient_rows=output_gradient_rows, factor_in=factor_in, factor_out=factor_out, list_counts=list_counts, list_seqs=list_seqs)


def reference(activations, output_gradient_rows, factor_in, factor_out, list_counts, list_seqs):
    input_projection_matrix = factor_in.reshape(QW * RANK, FF)
    output_projection_matrix = factor_out.reshape(QW * RANK, D)

    def project(pair):
        act_seq, grad_seq = pair
        inner_factor_basis = jnp.dot(act_seq, input_projection_matrix.T, preferred_element_type=jnp.float32)
        outer_factor_basis = jnp.dot(grad_seq, output_projection_matrix.T, preferred_element_type=jnp.float32)
        return (inner_factor_basis, outer_factor_basis)
    inner_factor_basis, outer_factor_basis = lax.map(project, (activations, output_gradient_rows))
    inner_factor_basis = inner_factor_basis.reshape(NSEQ, SEQ_LEN, QW, RANK)
    outer_factor_basis = outer_factor_basis.reshape(NSEQ, SEQ_LEN, QW, RANK)
    query_grid = jnp.broadcast_to(jnp.arange(QW, dtype=jnp.int32)[:, None], (QW, KMAX))
    seq_grid = list_seqs.astype(jnp.int32)
    picked_in = inner_factor_basis[seq_grid, :, query_grid, :]
    picked_out = outer_factor_basis[seq_grid, :, query_grid, :]
    raw = lax.optimization_barrier(jnp.sum(picked_in * picked_out, axis=3))
    valid = jnp.arange(KMAX, dtype=jnp.int32)[None, :] < list_counts[:, None]
    raw = jnp.where(valid[:, :, None], raw, jnp.float32(0.0))
    scores = jnp.transpose(raw, (2, 0, 1)).reshape(SEQ_LEN, QW * KMAX)
    sums = lax.optimization_barrier(jnp.sum(raw, axis=(1, 2)))
    totals = sums / jnp.sqrt((SEQ_LEN * list_counts).astype(jnp.float32))
    return (scores, totals)
```

```python
import functools

import jax
import jax.numpy as jnp
import numpy as np
from jax import lax
from jax.experimental import pallas as pl
from jax.experimental.pallas import tpu as pltpu
from jax.sharding import PartitionSpec as P

PAIRS = 40
GROUP = 8
CHUNKS = (2, 3)


def stage_bits(devices, core):
    count = devices.bit_length() - 1
    bits = list(range(count))
    if core and count > 2:
        bits[1], bits[2] = bits[2], bits[1]
    return bits


def stage_pairs(devices, stage):
    return [(i, i ^ (1 << stage_bits(devices, i & 1)[stage])) for i in range(devices)]


def block_order(devices):
    half = devices // 2
    table = np.zeros((devices, devices), np.int32)
    for me in range(devices):
        for part in range(2):
            owner = me ^ part
            bits = stage_bits(devices, owner & 1)[1:]
            for i in range(half):
                block = owner
                for position, bit in enumerate(reversed(bits)):
                    if i >> position & 1:
                        block ^= 1 << bit
                table[me, part * half + i] = block
    return table


def token_block(acc, block, rows):
    if rows % 8 == 0:
        return acc[pl.ds(pl.multiple_of(block * rows, rows), rows), :]
    share = 8 // rows
    tile = acc[pl.ds(pl.multiple_of(block // share * 8, 8), 8), :]
    found = tile[:rows]
    for i in range(1, share):
        found = jnp.where(lax.rem(block, share) == i, tile[i * rows : (i + 1) * rows], found)
    return found


def project_kernel(base, slots, max_list, rank, info, act, grad, fin, fout, keep, send, fin_g, fout_g, acc):
    step = pl.program_id(0)
    lane_pair = lax.rem(step, GROUP)
    width = GROUP * rank
    seq = info[base + step] // slots
    before = info[base + jnp.maximum(step - 1, 0)] // slots

    @pl.when(lane_pair == 0)
    def _():
        for j in range(GROUP):
            query = lax.rem(info[base + step + j], slots) // max_list
            fin_g[j * rank : (j + 1) * rank, :] = fin[query]
            fout_g[j * rank : (j + 1) * rank, :] = fout[query]

    @pl.when((lane_pair == 0) | (seq != before))
    def _():
        dims = (((1,), (1,)), ((), ()))
        inner = lax.dot_general(act[0], fin_g[...], dims, preferred_element_type=jnp.float32)
        outer = lax.dot_general(grad[0], fout_g[...], dims, preferred_element_type=jnp.float32)
        live = lax.broadcasted_iota(jnp.int32, inner.shape, 1) >= lane_pair * rank
        acc[:, :width] = jnp.where(live, inner, acc[:, :width])
        acc[:, width:] = jnp.where(live, outer, acc[:, width:])

    @pl.when(lane_pair == GROUP - 1)
    def _():
        blocks = info.shape[0] - PAIRS
        rows = acc.shape[0] // blocks
        for i in range(blocks // 2):
            keep[i * rows : (i + 1) * rows, :] = token_block(acc, info[PAIRS + i], rows)
            send[i * rows : (i + 1) * rows, :] = token_block(acc, info[PAIRS + blocks // 2 + i], rows)


def project(first_group, groups, info, activations, output_gradient_rows, factor_in, factor_out, max_list):
    _, tokens, width_in = activations.shape
    width_out = output_gradient_rows.shape[2]
    queries, rank, _ = factor_in.shape
    base = first_group * GROUP
    slots = queries * max_list
    columns = 2 * GROUP * rank

    def seq_block(step, info):
        return (info[base + step] // slots, 0, 0)

    out = jax.ShapeDtypeStruct((tokens // 2, groups * columns), jnp.float32)
    out_spec = pl.BlockSpec((tokens // 2, columns), lambda step, info: (0, step // GROUP))
    return pl.pallas_call(
        functools.partial(project_kernel, base, slots, max_list, rank),
        grid_spec=pltpu.PrefetchScalarGridSpec(
            num_scalar_prefetch=1,
            grid=(groups * GROUP,),
            in_specs=[
                pl.BlockSpec((1, tokens, width_in), seq_block),
                pl.BlockSpec((1, tokens, width_out), seq_block),
                pl.BlockSpec((queries, rank, width_in), lambda step, info: (0, 0, 0)),
                pl.BlockSpec((queries, rank, width_out), lambda step, info: (0, 0, 0)),
            ],
            out_specs=[out_spec, out_spec],
            scratch_shapes=[
                pltpu.VMEM((GROUP * rank, width_in), jnp.bfloat16),
                pltpu.VMEM((GROUP * rank, width_out), jnp.bfloat16),
                pltpu.VMEM((tokens, columns), jnp.float32),
            ],
        ),
        out_shape=[out, out],
        compiler_params=pltpu.CompilerParams(vmem_limit_bytes=40 * 1024 * 1024),
        name="project",
    )(info, activations, output_gradient_rows, factor_in, factor_out)


def per_device(activations, output_gradient_rows, factor_in, factor_out, list_counts, list_seqs):
    tokens = activations.shape[1]
    queries, rank, _ = factor_in.shape
    max_list = list_seqs.shape[1]
    devices = lax.axis_size("tensor")
    stages = devices.bit_length() - 1
    rows = tokens // devices
    slots = queries * max_list

    slot = jnp.arange(slots, dtype=jnp.int32)
    valid = (jnp.arange(max_list, dtype=jnp.int32)[None, :] < list_counts[:, None]).reshape(-1)
    key = jnp.where(valid, list_seqs.reshape(-1), activations.shape[0]) * slots + slot
    place = jnp.sum((key[None, :] < key[:, None]).astype(jnp.int32), axis=1)
    pair = jnp.arange(PAIRS, dtype=jnp.int32)
    ordered = jnp.sum(jnp.where(place[:, None] == pair[None, :], key[:, None], 0), axis=0)
    order = jnp.asarray(block_order(devices))[lax.axis_index("tensor")]
    info = jnp.concatenate([ordered, order])

    products = []
    first = 0
    for groups in CHUNKS:
        keep, send = project(
            first, groups, info, activations, output_gradient_rows, factor_in, factor_out, max_list
        )
        first += groups
        for stage in range(stages):
            got = lax.ppermute(send, "tensor", stage_pairs(devices, stage))
            if stage < stages - 1:
                half = keep.shape[0] // 2
                send = keep[half:] + got[half:]
                keep = keep[:half] + got[:half]
            else:
                keep = keep + got
        basis = keep.reshape(rows, groups, 2, GROUP * rank)
        products.append((basis[:, :, 0] * basis[:, :, 1]).reshape(rows, groups * GROUP * rank))
    product = jnp.concatenate(products, axis=1)
    slot_of = jnp.repeat(lax.rem(ordered, slots), rank)
    spread = (slot_of[:, None] == slot[None, :]).astype(jnp.float32)
    scores = jnp.dot(product, spread, precision=lax.Precision.HIGHEST)
    sums = jnp.sum(scores.reshape(rows, queries, max_list), axis=(0, 2))
    for stage in range(stages):
        sums = sums + lax.ppermute(sums, "tensor", stage_pairs(devices, stage))
    totals = sums / jnp.sqrt((tokens * list_counts).astype(jnp.float32))
    return (scores, totals)


def solution(mesh):
    in_specs = (
        P("runs", None, "tensor"),
        P("runs", None, "tensor"),
        P("runs", None, "tensor"),
        P("runs", None, "tensor"),
        P("runs"),
        P("runs", None),
    )
    out_specs = (P("tensor", "runs"), P("runs"))
    return jax.shard_map(
        per_device, mesh=mesh, in_specs=in_specs, out_specs=out_specs, check_vma=False
    )
```

```python
import functools

import jax
import jax.numpy as jnp
import numpy as np
from jax import lax
from jax.experimental import pallas as pl
from jax.experimental.pallas import tpu as pltpu
from jax.sharding import PartitionSpec as P

PAIRS = 40
GROUP = 8
CHUNKS = (2, 3)
BUFFERS = 4


def stage_bits(devices, core):
    count = devices.bit_length() - 1
    bits = list(range(count))
    if core and count > 2:
        bits[1], bits[2] = bits[2], bits[1]
    return bits


def stage_pairs(devices, stage):
    return [(i, i ^ (1 << stage_bits(devices, i & 1)[stage])) for i in range(devices)]


def block_order(devices):
    half = devices // 2
    table = np.zeros((devices, devices), np.int32)
    for me in range(devices):
        for part in range(2):
            owner = me ^ part
            bits = stage_bits(devices, owner & 1)[1:]
            for i in range(half):
                block = owner
                for position, bit in enumerate(reversed(bits)):
                    if i >> position & 1:
                        block ^= 1 << bit
                table[me, part * half + i] = block
    return table


def token_block(acc, block, rows):
    if rows % 8 == 0:
        return acc[pl.ds(pl.multiple_of(block * rows, rows), rows), :]
    share = 8 // rows
    tile = acc[pl.ds(pl.multiple_of(block // share * 8, 8), 8), :]
    found = tile[:rows]
    for i in range(1, share):
        found = jnp.where(lax.rem(block, share) == i, tile[i * rows : (i + 1) * rows], found)
    return found


def project_kernel(base, info, act, grad, fin, fout, keep, send, *scratch):
    acts, grads, fins, fouts, acc, todo, act_sem, grad_sem, fin_sem, fout_sem = scratch
    rank = fins.shape[2]
    buffers = acts.shape[0]
    tokens, columns = acc.shape
    width = columns // 2
    pairs = keep.shape[1] // columns * GROUP
    blocks = info.shape[0] - 2 * PAIRS
    rows = tokens // blocks

    def is_new(pair):
        return (pair == 0) | (info[base + pair] != info[base + jnp.maximum(pair - 1, 0)])

    def list_new(pair, count):
        new = is_new(pair)

        @pl.when(new)
        def _():
            todo[count] = info[base + pair]

        return count + new.astype(jnp.int32)

    def sequence_copies(index):
        buffer = lax.rem(index, buffers)
        return (
            pltpu.make_async_copy(act.at[todo[index]], acts.at[buffer], act_sem.at[buffer]),
            pltpu.make_async_copy(grad.at[todo[index]], grads.at[buffer], grad_sem.at[buffer]),
        )

    def fetch_sequence(index):
        for copy in sequence_copies(index):
            copy.start()

    def fetch_factors(group):
        half = lax.rem(group, 2)
        for i in range(GROUP):
            query = info[PAIRS + base + group * GROUP + i]
            pltpu.make_async_copy(fin.at[query], fins.at[half, i], fin_sem.at[half]).start()
            pltpu.make_async_copy(fout.at[query], fouts.at[half, i], fout_sem.at[half]).start()

    def wait_factors(group):
        half = lax.rem(group, 2)
        pltpu.make_async_copy(fin.at[pl.ds(0, GROUP)], fins.at[half], fin_sem.at[half]).wait()
        pltpu.make_async_copy(fout.at[pl.ds(0, GROUP)], fouts.at[half], fout_sem.at[half]).wait()

    fetch_factors(0)
    count = lax.fori_loop(0, pairs, list_new, 0)
    for i in range(buffers - 1):
        pl.when(i < count)(functools.partial(fetch_sequence, i))

    def one_pair(pair, index):
        lane_pair = lax.rem(pair, GROUP)
        group = pair // GROUP
        half = lax.rem(group, 2)
        new = is_new(pair)
        index = index + new.astype(jnp.int32)
        buffer = lax.rem(index, buffers)

        @pl.when(lane_pair == 0)
        def _():
            wait_factors(group)
            pl.when(group + 1 < pairs // GROUP)(lambda: fetch_factors(group + 1))

        @pl.when(new)
        def _():
            for copy in sequence_copies(index):
                copy.wait()
            pl.when(index + buffers - 1 < count)(lambda: fetch_sequence(index + buffers - 1))

        @pl.when((lane_pair == 0) | new)
        def _():
            dims = (((1,), (1,)), ((), ()))
            live = lax.broadcasted_iota(jnp.int32, (tokens, width), 1) >= lane_pair * rank
            for x, factors, lanes in ((acts, fins, slice(0, width)), (grads, fouts, slice(width, columns))):
                basis = lax.dot_general(
                    x[buffer],
                    factors[half].reshape(width, factors.shape[3]),
                    dims,
                    preferred_element_type=jnp.float32,
                )
                acc[:, lanes] = jnp.where(live, basis, acc[:, lanes])

        @pl.when(lane_pair == GROUP - 1)
        def _():
            lanes = pl.ds(pl.multiple_of(group * columns, columns), columns)
            for i in range(blocks // 2):
                here = slice(i * rows, (i + 1) * rows)
                keep[here, lanes] = token_block(acc, info[2 * PAIRS + i], rows)
                send[here, lanes] = token_block(acc, info[2 * PAIRS + blocks // 2 + i], rows)

        return index

    lax.fori_loop(0, pairs, one_pair, -1)


def project(first_group, groups, info, activations, output_gradient_rows, factor_in, factor_out):
    _, tokens, width_in = activations.shape
    width_out = output_gradient_rows.shape[2]
    rank = factor_in.shape[1]
    arrays = (activations, output_gradient_rows, factor_in, factor_out)
    columns = 2 * GROUP * rank
    out = jax.ShapeDtypeStruct((tokens // 2, groups * columns), jnp.float32)
    return pl.pallas_call(
        functools.partial(project_kernel, first_group * GROUP),
        in_specs=[pl.BlockSpec(memory_space=pltpu.SMEM)] + [pl.BlockSpec(memory_space=pltpu.HBM)] * 4,
        out_specs=[pl.BlockSpec(memory_space=pltpu.VMEM)] * 2,
        scratch_shapes=[
            pltpu.VMEM((BUFFERS, tokens, width_in), jnp.bfloat16),
            pltpu.VMEM((BUFFERS, tokens, width_out), jnp.bfloat16),
            pltpu.VMEM((2, GROUP, rank, width_in), jnp.bfloat16),
            pltpu.VMEM((2, GROUP, rank, width_out), jnp.bfloat16),
            pltpu.VMEM((tokens, columns), jnp.float32),
            pltpu.SMEM((PAIRS,), jnp.int32),
            pltpu.SemaphoreType.DMA((BUFFERS,)),
            pltpu.SemaphoreType.DMA((BUFFERS,)),
            pltpu.SemaphoreType.DMA((2,)),
            pltpu.SemaphoreType.DMA((2,)),
        ],
        out_shape=[out, out],
        compiler_params=pltpu.CompilerParams(vmem_limit_bytes=24 * 1024 * 1024),
        name="project",
    )(info, *[pltpu.with_memory_space_constraint(x, pltpu.HBM) for x in arrays])


def per_device(activations, output_gradient_rows, factor_in, factor_out, list_counts, list_seqs):
    tokens = activations.shape[1]
    queries, rank, _ = factor_in.shape
    max_list = list_seqs.shape[1]
    devices = lax.axis_size("tensor")
    stages = devices.bit_length() - 1
    rows = tokens // devices
    slots = queries * max_list

    slot = jnp.arange(slots, dtype=jnp.int32)
    valid = (jnp.arange(max_list, dtype=jnp.int32)[None, :] < list_counts[:, None]).reshape(-1)
    key = jnp.where(valid, list_seqs.reshape(-1), activations.shape[0]) * slots + slot
    place = jnp.sum((key[None, :] < key[:, None]).astype(jnp.int32), axis=1)
    pair = jnp.arange(PAIRS, dtype=jnp.int32)
    ordered = jnp.sum(jnp.where(place[:, None] == pair[None, :], key[:, None], 0), axis=0)
    order = jnp.asarray(block_order(devices))[lax.axis_index("tensor")]
    info = jnp.concatenate([ordered // slots, lax.rem(ordered, slots) // max_list, order])

    products = []
    first = 0
    for groups in CHUNKS:
        keep, send = project(
            first, groups, info, activations, output_gradient_rows, factor_in, factor_out
        )
        first += groups
        for stage in range(stages):
            got = lax.ppermute(send, "tensor", stage_pairs(devices, stage))
            if stage < stages - 1:
                half = keep.shape[0] // 2
                send = keep[half:] + got[half:]
                keep = keep[:half] + got[:half]
            else:
                keep = keep + got
        basis = keep.reshape(rows, groups, 2, GROUP * rank)
        products.append((basis[:, :, 0] * basis[:, :, 1]).reshape(rows, groups * GROUP * rank))
    product = jnp.concatenate(products, axis=1)
    slot_of = jnp.repeat(lax.rem(ordered, slots), rank)
    spread = (slot_of[:, None] == slot[None, :]).astype(jnp.float32)
    scores = jnp.dot(product, spread, precision=lax.Precision.HIGHEST)
    sums = jnp.sum(scores.reshape(rows, queries, max_list), axis=(0, 2))
    for stage in range(stages):
        sums = sums + lax.ppermute(sums, "tensor", stage_pairs(devices, stage))
    totals = sums / jnp.sqrt((tokens * list_counts).astype(jnp.float32))
    return (scores, totals)


def solution(mesh):
    in_specs = (
        P("runs", None, "tensor"),
        P("runs", None, "tensor"),
        P("runs", None, "tensor"),
        P("runs", None, "tensor"),
        P("runs"),
        P("runs", None),
    )
    out_specs = (P("tensor", "runs"), P("runs"))
    return jax.shard_map(
        per_device, mesh=mesh, in_specs=in_specs, out_specs=out_specs, check_vma=False
    )
```

```python
import functools

import jax
import jax.numpy as jnp
from jax import lax
from jax.experimental import pallas as pl
from jax.experimental.pallas import tpu as pltpu
from jax.sharding import PartitionSpec as P

PAIRS = 40
GROUP = 8
CHUNKS = (3, 2)
VMEM_LIMIT = 4 * 1024 * 1024
SCORE_FLOPS = 1000000
BUFFERS = 4
READ, READ_OF, SLOT = range(3)


def stage_bits(devices, core):
    count = devices.bit_length() - 1
    bits = list(range(count))
    if core and count > 2:
        bits[1], bits[2] = bits[2], bits[1]
    return bits


def stage_pairs(devices, stage):
    return [(i, i ^ (1 << stage_bits(devices, i & 1)[stage])) for i in range(devices)]


def block_offset(devices, core, position):
    bits = stage_bits(devices, core)[1:]
    return sum(1 << bit for i, bit in enumerate(reversed(bits)) if position >> i & 1)


def token_block(acc, block, rows):
    if rows % 8 == 0:
        return acc[pl.ds(pl.multiple_of(block * rows, rows), rows), :]
    share = 8 // rows
    tile = acc[pl.ds(pl.multiple_of(block // share * 8, 8), 8), :]
    found = tile[:rows]
    for i in range(1, share):
        found = jnp.where(lax.rem(block, share) == i, tile[i * rows : (i + 1) * rows], found)
    return found


def project_kernel(base, pairs, devices, max_list, *refs):
    if base == 0:
        order, act, grad, fin, fout, *rest = refs
        keep, send, plan, acts, grads, fins, fouts, acc, act_sem, grad_sem, fin_sem, fout_sem = rest
    else:
        plan, act, grad, fin, fout, *rest = refs
        _, _, _, _, keep, send, acts, grads, fins, fouts, acc, act_sem, grad_sem, fin_sem, fout_sem = rest
    rank = fins.shape[2]
    tokens, columns = acc.shape
    width = columns // 2
    rows = tokens // devices
    last = base + pairs == PAIRS
    me = lax.axis_index("tensor")

    def copies_to(buffer, seq):
        return (
            pltpu.make_async_copy(act.at[seq], acts.at[buffer], act_sem.at[buffer]),
            pltpu.make_async_copy(grad.at[seq], grads.at[buffer], grad_sem.at[buffer]),
        )

    def fetch(read):
        for copy in copies_to(lax.rem(read, BUFFERS), plan[READ, read]):
            copy.start()

    def wait(read):
        for copy in copies_to(lax.rem(read, BUFFERS), plan[READ, read]):
            copy.wait()

    def fetch_factors(group):
        half = lax.rem(group, 2)
        for i in range(GROUP):
            query = plan[SLOT, group * GROUP + i] // max_list
            pltpu.make_async_copy(fin.at[query], fins.at[half, i], fin_sem.at[half]).start()
            pltpu.make_async_copy(fout.at[query], fouts.at[half, i], fout_sem.at[half]).start()

    def wait_factors(group):
        half = lax.rem(group, 2)
        pltpu.make_async_copy(fin.at[pl.ds(0, GROUP)], fins.at[half], fin_sem.at[half]).wait()
        pltpu.make_async_copy(fout.at[pl.ds(0, GROUP)], fouts.at[half], fout_sem.at[half]).wait()

    if base == 0:
        for copy in copies_to(0, order[0]):
            copy.start()
        for i in range(GROUP):
            plan[SLOT, i] = order[PAIRS + i]
        fetch_factors(0)

        def number(pair, carry):
            read, before = carry
            seq = order[pair]
            new = seq != before
            read = read + new.astype(jnp.int32)
            plan[READ, read] = seq
            plan[READ_OF, pair] = read
            plan[SLOT, pair] = order[PAIRS + pair]
            pl.when(new & (read > 0) & (read < BUFFERS - 1))(lambda: fetch(read))
            return read, seq

        lax.fori_loop(0, PAIRS, number, (-1, -1))
        begin, held = -1, -1
    else:
        begin = plan[READ_OF, base - 1]
        held = begin + BUFFERS - 2
    reads = plan[READ_OF, PAIRS - 1] + 1
    end = reads if last else plan[READ_OF, base + pairs - 1]
    if base > 0:
        pl.when(held + 1 < reads)(lambda: fetch(held + 1))

    def one_pair(pair, before):
        lane_pair = lax.rem(pair, GROUP)
        group = pair // GROUP
        half = lax.rem(group, 2)
        read = plan[READ_OF, pair]
        new = read != before
        buffer = lax.rem(read, BUFFERS)

        @pl.when(lane_pair == 0)
        def _():
            pl.when((group > base // GROUP) | (base == 0))(lambda: wait_factors(group))
            pl.when(group + 1 < PAIRS // GROUP)(lambda: fetch_factors(group + 1))

        @pl.when(new)
        def _():
            pl.when(read > held)(lambda: wait(read))
            pl.when((read + BUFFERS - 1 < reads) & (read != end))(lambda: fetch(read + BUFFERS - 1))

        @pl.when((lane_pair == 0) | new)
        def _():
            dims = (((1,), (1,)), ((), ()))
            live = lax.broadcasted_iota(jnp.int32, (tokens, width), 1) >= lane_pair * rank
            for x, factors, lanes in ((acts, fins, slice(0, width)), (grads, fouts, slice(width, columns))):
                basis = lax.dot_general(
                    x[buffer],
                    factors[half].reshape(width, factors.shape[3]),
                    dims,
                    preferred_element_type=jnp.float32,
                )
                acc[:, lanes] = jnp.where(live, basis, acc[:, lanes])

        @pl.when(lane_pair == GROUP - 1)
        def _():
            start = pl.multiple_of((group - base // GROUP) * columns, columns)
            lanes = pl.ds(start, columns)
            core = me & 1
            for i in range(devices // 2):
                here = slice(i * rows, (i + 1) * rows)
                offsets = [block_offset(devices, c, i) for c in range(2)]
                kept = me ^ jnp.where(core == 0, *offsets)
                sent = me ^ 1 ^ jnp.where(core == 1, *offsets)
                keep[here, lanes] = token_block(acc, kept, rows)
                send[here, lanes] = token_block(acc, sent, rows)

        return read

    lax.fori_loop(base, base + pairs, one_pair, begin)
    if not last:
        wait_factors((base + pairs) // GROUP)
        for i in range(1, BUFFERS - 1):
            pl.when((end + i < reads) & (end + i > held))(functools.partial(wait, end + i))


def project(first_group, groups, devices, max_list, plan, arrays, buffers):
    _, tokens, width_in = arrays[0].shape
    width_out = arrays[1].shape[2]
    rank = arrays[2].shape[1]
    columns = 2 * GROUP * rank
    smem, vmem = pl.BlockSpec(memory_space=pltpu.SMEM), pl.BlockSpec(memory_space=pltpu.VMEM)
    out = [jax.ShapeDtypeStruct((tokens // 2, groups * columns), jnp.float32)] * 2
    out_specs = [vmem] * 2
    scratch = [pltpu.VMEM((tokens, columns), jnp.float32)]
    aliases = {}
    if first_group == 0:
        out.append(jax.ShapeDtypeStruct((3, PAIRS), jnp.int32))
        out_specs.append(smem)
    else:
        aliases = {1 + len(arrays) + i: 2 + i for i in range(len(buffers))}
    out += [jax.ShapeDtypeStruct(shape, jnp.bfloat16) for shape in buffer_shapes(arrays)]
    out_specs += [vmem] * 4
    return pl.pallas_call(
        functools.partial(project_kernel, first_group * GROUP, groups * GROUP, devices, max_list),
        in_specs=[smem] + [pl.BlockSpec(memory_space=pltpu.HBM)] * 4 + [vmem] * len(buffers),
        out_specs=out_specs,
        scratch_shapes=scratch
        + [
            pltpu.SemaphoreType.DMA((BUFFERS,)),
            pltpu.SemaphoreType.DMA((BUFFERS,)),
            pltpu.SemaphoreType.DMA((2,)),
            pltpu.SemaphoreType.DMA((2,)),
        ],
        out_shape=out,
        input_output_aliases=aliases,
        compiler_params=pltpu.CompilerParams(vmem_limit_bytes=VMEM_LIMIT),
        cost_estimate=pl.CostEstimate(
            flops=groups * GROUP * columns * tokens * (width_in + width_out),
            bytes_accessed=groups * GROUP * 2 * tokens * (width_in + width_out),
            transcendentals=0,
        ),
        name="project",
    )(plan, *[pltpu.with_memory_space_constraint(x, pltpu.HBM) for x in arrays], *buffers)


def buffer_shapes(arrays):
    sequences, factors = [x.shape[1:] for x in arrays[:2]], [x.shape[1:] for x in arrays[2:]]
    return [(BUFFERS, *s) for s in sequences] + [(2, GROUP, *s) for s in factors]


def per_device(activations, output_gradient_rows, factor_in, factor_out, list_counts, list_seqs):
    tokens = activations.shape[1]
    queries, rank, _ = factor_in.shape
    max_list = list_seqs.shape[1]
    devices = lax.axis_size("tensor")
    stages = devices.bit_length() - 1
    rows = tokens // devices
    slots = queries * max_list
    arrays = (activations, output_gradient_rows, factor_in, factor_out)

    def send_on(stage, send):
        return lax.ppermute(send, "tensor", stage_pairs(devices, stage))

    def halve(keep, got):
        half = keep.shape[0] // 2
        return keep[:half] + got[:half], keep[half:] + got[half:]

    slot = jnp.arange(slots, dtype=jnp.int32)
    listed = (jnp.arange(max_list, dtype=jnp.int32)[None, :] < list_counts[:, None]).reshape(-1)
    key = jnp.where(listed, list_seqs.reshape(-1), activations.shape[0]) * slots + slot
    place = jnp.sum((key[None, :] < key[:, None]).astype(jnp.int32), axis=1)
    pair = jnp.arange(PAIRS, dtype=jnp.int32)
    ordered = jnp.sum(jnp.where(place[:, None] == pair[None, :], key[:, None], 0), axis=0)
    slot_of = lax.rem(ordered, slots)
    plan = jnp.concatenate([ordered // slots, slot_of])

    buffers, flights = [], []
    first = 0
    for groups in CHUNKS:
        gots = [send_on(stage, send) for stage, _, send in flights]
        made = project(first, groups, devices, max_list, plan, arrays, buffers)
        (keep, send, *made), gots = lax.optimization_barrier((made, gots))
        if first == 0:
            plan, *buffers = made
        else:
            buffers = made
        first += groups
        flights = [(stage + 1, *halve(kept, got)) for (stage, kept, _), got in zip(flights, gots)]
        flights.append((1, *halve(keep, send_on(0, send))))
        plan, _ = lax.optimization_barrier((plan, [send for _, _, send in flights]))
    products = []
    for groups, (reached, keep, send) in zip(CHUNKS, flights):
        for stage in range(reached, stages - 1):
            keep, send = halve(keep, send_on(stage, send))
        keep = keep + send_on(stages - 1, send)
        basis = keep.reshape(rows, groups, 2, GROUP * rank)
        products.append((basis[:, :, 0] * basis[:, :, 1]).reshape(rows, groups * GROUP * rank))
    product = jnp.concatenate(products, axis=1)
    spread = (jnp.repeat(slot_of, rank)[:, None] == slot[None, :]).astype(jnp.float32)
    scores = jnp.dot(product, spread, precision=lax.Precision.HIGHEST)
    sums = jnp.sum(scores.reshape(rows, queries, max_list), axis=(0, 2))
    for stage in range(stages):
        sums = sums + send_on(stage, sums)
    totals = sums / jnp.sqrt((tokens * list_counts).astype(jnp.float32))
    return (scores, totals)


def solution(mesh):
    in_specs = (
        P("runs", None, "tensor"),
        P("runs", None, "tensor"),
        P("runs", None, "tensor"),
        P("runs", None, "tensor"),
        P("runs"),
        P("runs", None),
    )
    out_specs = (P("tensor", "runs"), P("runs"))
    return jax.shard_map(
        per_device, mesh=mesh, in_specs=in_specs, out_specs=out_specs, check_vma=False
    )
```
